128 devices in a mesh: row: 8 (over x_lo, z), col: 16 (over y, x_hi, core).
Axes of the slice: x: 4 (x_hi: 2, x_lo: 2; x = x_hi * 2 + x_lo), y: 4, z: 4, core: 2. Of those that a mesh axis runs over, the one named last changes fastest.
Arguments:
- unfolding: bfloat16 [6144, 4096], P('row', 'col'), may hold values from -400 to 400
Outputs:
- regrouped: bfloat16 [256, 16, 6144], P('col', None, 'row')
The draws below stay inside these ranges and needn't reach their ends.
All inputs are finite; a program needn't handle non-finite values.
Results may differ from the reference program's by a relative error of at most 0.0062.
Values may be sent and summed in bfloat16 or wider, within the bound.
No kernel may reach another device: no remote copies, remote signals or barrier semaphores. Data moves between devices by JAX's collectives and lax.ppermute only.
A program may use at most 64 MiB of HBM per device.

```python
import math
import jax
import jax.numpy as jnp

VIEWS = 16
PIXELS = 256
ITERS = 2
ROWS_DEV = 768
COLS = 4096
ROWS = 6144


def draw_unfolding(key, part):
    keys = jax.random.split(jax.random.fold_in(key, 11), 7)
    block_count = ROWS // ROWS_DEV
    block_order = jax.random.permutation(keys[3], block_count).astype(jnp.float32) / max(block_count - 1, 1)
    view_order = jax.random.permutation(keys[4], VIEWS).astype(jnp.float32) / max(VIEWS - 1, 1)
    row_block = block_order[jnp.arange(ROWS) // ROWS_DEV]
    col_block = view_order[jnp.arange(COLS) // PIXELS]
    row_scale = 3.0 ** row_block * jnp.exp(jax.random.uniform(keys[1], (ROWS,), jnp.float32) * math.log(10.0 / 3.0))
    spike_rank = 16
    targets = [0.4 + 1.0 * step / (spike_rank - 1) for step in range(spike_rank)]
    denominator = COLS - 9.0 * sum(targets)
    left_vectors = jax.random.normal(keys[5], (ROWS, spike_rank), jnp.float32)
    right_vectors = jax.random.normal(keys[6], (COLS, spike_rank), jnp.float32)
    spikes = jnp.zeros((ROWS, COLS), jnp.float32)
    for step in range(spike_rank):
        amplitude = math.sqrt(9.0 * targets[step] / denominator)
        spikes = spikes + (amplitude * left_vectors[:, step])[:, None] * right_vectors[:, step][None, :]
    base = jax.random.normal(keys[0], (ROWS, COLS), jnp.float32)
    col_scale = 3.0 ** col_block * jnp.exp(jax.random.uniform(keys[2], (COLS,), jnp.float32) * math.log(10.0 / 3.0))
    inner = jnp.clip(base + spikes, -4.0, 4.0)
    return (inner * row_scale[:, None] * col_scale[None, :]).astype(jnp.bfloat16)


def setup_inputs(seed: int = 0) -> dict:
    key_list = jax.random.split(jax.random.key(seed), 2)
    return {
        "unfolding": draw_unfolding(jax.random.fold_in(key_list[1], 71), 0),
    }


def reference(unfolding):
    values = unfolding.astype(jnp.float32)
    sumsq = jnp.sum(values * values)
    current = (values * (math.sqrt(COLS) / (3.0 * jnp.sqrt(sumsq)))).astype(jnp.bfloat16)
    updated = current.astype(jnp.float32)
    for turn_index in range(ITERS):
        gram = jnp.dot(current.T, current, preferred_element_type=jnp.float32).astype(jnp.bfloat16)
        first = jnp.dot(current, gram, preferred_element_type=jnp.float32).astype(jnp.bfloat16)
        second = jnp.dot(first, gram, preferred_element_type=jnp.float32)
        updated = 1.875 * current.astype(jnp.float32) - 1.25 * first.astype(jnp.float32) + 0.375 * second
        if turn_index + 1 < ITERS:
            current = updated.astype(jnp.bfloat16)
    final = updated * math.sqrt(ROWS)
    cube = final.reshape(ROWS, VIEWS, PIXELS).transpose(2, 1, 0)
    return cube.astype(jnp.bfloat16)
```

```python
import math

import jax
import jax.numpy as jnp
from jax import lax
from jax.sharding import Mesh
from jax.sharding import PartitionSpec as P

ITERS = 2
ROWS = 6144
COLS = 4096
BF = jnp.bfloat16
F32 = jnp.float32

AXES = ("xlo", "z", "y", "xhi", "core")


def pairs(move):
    out = []
    for xlo in range(2):
        for z in range(4):
            for y in range(4):
                for xhi in range(2):
                    for c in range(2):
                        x = 2 * xhi + xlo
                        x2, y2, z2, c2 = move(x, y, z, c)
                        x2, y2, z2, c2 = x2 % 4, y2 % 4, z2 % 4, c2 % 2
                        src = (((xlo * 4 + z) * 4 + y) * 2 + xhi) * 2 + c
                        dst = ((((x2 % 2) * 4 + z2) * 4 + y2) * 2 + x2 // 2) * 2 + c2
                        out.append((src, dst))
    return out


def permute(value, move):
    return lax.ppermute(value, AXES, pairs(move))


def swap_cores(value):
    return permute(value, lambda x, y, z, c: (x, y, z, 1 - c))


def from_y(value, j):
    return permute(value, lambda x, y, z, c: (x, y - j, z, c))


def to_major(value, d):
    return permute(value, lambda x, y, z, c: (x + d, y, z, c) if c == 0 else (x, y, z + d, c))


def to_minor(value, d):
    return permute(value, lambda x, y, z, c: (x, y, z + d, c) if c == 0 else (x + d, y, z, c))


def dot(a, b):
    return jnp.dot(a, b, preferred_element_type=F32)


def dot_t(a, b):
    return lax.dot_general(a, b, (((0,), (0,)), ((), ())), preferred_element_type=F32)


def gather_columns(block):
    arrived = {0: block}
    for j in (1, 3, 2):
        arrived[j] = from_y(block, j)
    return [jnp.concatenate([arrived[j], swap_cores(arrived[j])], axis=1) for j in range(4)]


def rows_at(value, index, size):
    return lax.dynamic_slice_in_dim(value, index * size, size, 0)


def place(blocks, first):
    size = blocks[0].shape[0]
    out = jnp.zeros((4 * size,) + blocks[0].shape[1:], blocks[0].dtype)
    for e, block in enumerate(blocks):
        out = lax.dynamic_update_slice_in_dim(out, block, ((first + e) % 4) * size, 0)
    return out


def local(unfolding):
    x_hi = lax.axis_index("xhi")
    x = 2 * x_hi + lax.axis_index("xlo")
    z = lax.axis_index("z")
    core = lax.axis_index("core")
    major = jnp.where(core == 0, x, z)
    minor = jnp.where(core == 0, z, x)

    half = unfolding.shape[0] // 2
    values = unfolding.astype(F32)
    sums = lax.psum(jnp.sum(values * values), AXES)
    factor = math.sqrt(COLS) / (3.0 * jnp.sqrt(sums))

    mine = lax.dynamic_slice_in_dim(unfolding, x_hi * half, half, 0)
    other = permute(
        lax.dynamic_slice_in_dim(unfolding, (1 - x_hi) * half, half, 0),
        lambda x, y, z, c: (x + 2, y, z, c),
    )
    current = jnp.concatenate(
        [jnp.where(x_hi == 0, mine, other), jnp.where(x_hi == 0, other, mine)], axis=1
    )
    scale = factor
    for turn_index in range(ITERS):
        blocks = gather_columns(current)
        whole = jnp.concatenate(blocks, axis=1)
        width = blocks[0].shape[1]
        slices = [
            lax.dynamic_slice_in_dim(whole, ((major + d) % 4) * width, width, 1) for d in range(4)
        ]
        total = dot_t(slices[0], current)
        for d in (1, 3, 2):
            total = total + to_major(dot_t(slices[d], current).astype(BF), d).astype(F32)
        piece = total.shape[0] // 4
        share = rows_at(total, minor, piece)
        for e in (1, 3, 2):
            share = share + to_minor(rows_at(total, (minor + e) % 4, piece).astype(BF), e).astype(F32)
        share = (share * (scale * scale)).astype(BF)
        quarter = place([share] + [to_minor(share, -e) for e in (1, 2, 3)], minor)
        gram = [quarter] + [to_major(quarter, -d) for d in (1, 2, 3)]
        first = dot(slices[0], gram[0])
        for d in (1, 3, 2):
            first = first + dot(slices[d], gram[d])
        first = (first * scale).astype(BF)
        ordered = place(gram, major)
        firsts = gather_columns(first)
        second = dot(firsts[0], rows_at(ordered, 0, width))
        for j in (1, 3, 2):
            second = second + dot(firsts[j], rows_at(ordered, j, width))
        updated = (
            (1.875 * scale) * current.astype(F32) - 1.25 * first.astype(F32) + 0.375 * second
        )
        current = updated.astype(BF)
        scale = jnp.float32(1.0)

    final = (updated * math.sqrt(ROWS)).astype(BF)
    pixels = final.shape[1] // 2
    parts = final.reshape(half, 2, 16, pixels // 16).transpose(2, 3, 1, 0)
    parts = lax.all_to_all(parts, ("y", "xhi", "core"), split_axis=0, concat_axis=0, tiled=True)
    parts = parts.reshape(4, 2, 2, pixels // 16, 2, half).transpose(3, 0, 4, 2, 1, 5)
    return parts.reshape(pixels // 16, 16, 2 * half)


def solution(mesh):
    wide = Mesh(mesh.devices.reshape(2, 4, 4, 2, 2), AXES)
    return jax.shard_map(
        local,
        mesh=wide,
        in_specs=(P(("xlo", "z"), ("y", "xhi", "core")),),
        out_specs=P(("y", "xhi", "core"), None, ("xlo", "z")),
        check_vma=False,
    )
```

```python
import math

import jax
import jax.numpy as jnp
from jax import lax
from jax.sharding import Mesh
from jax.sharding import PartitionSpec as P

ITERS = 2
ROWS = 6144
COLS = 4096
BF = jnp.bfloat16
F32 = jnp.float32

AXES = ("xlo", "z", "y", "xhi", "core")


def pairs(move):
    out = []
    for xlo in range(2):
        for z in range(4):
            for y in range(4):
                for xhi in range(2):
                    for c in range(2):
                        x = 2 * xhi + xlo
                        x2, y2, z2, c2 = move(x, y, z, c)
                        x2, y2, z2, c2 = x2 % 4, y2 % 4, z2 % 4, c2 % 2
                        src = (((xlo * 4 + z) * 4 + y) * 2 + xhi) * 2 + c
                        dst = ((((x2 % 2) * 4 + z2) * 4 + y2) * 2 + x2 // 2) * 2 + c2
                        out.append((src, dst))
    return out


def permute(value, move):
    return lax.ppermute(value, AXES, pairs(move))


def swap_cores(value):
    return permute(value, lambda x, y, z, c: (x, y, z, 1 - c))


def from_y(value, j):
    return permute(value, lambda x, y, z, c: (x, y - j, z, c))


def to_major(value, d):
    return permute(value, lambda x, y, z, c: (x + d, y, z, c) if c == 0 else (x, y, z + d, c))


def to_minor(value, d):
    return permute(value, lambda x, y, z, c: (x, y, z + d, c) if c == 0 else (x + d, y, z, c))


def sum_over_all(value):
    for move in (
        lambda x, y, z, c: (x, y, z, 1 - c),
        lambda x, y, z, c: (x, y ^ 1, z, c),
        lambda x, y, z, c: (x, y ^ 2, z, c),
        lambda x, y, z, c: (x ^ 1, y, z, c),
        lambda x, y, z, c: (x ^ 2, y, z, c),
        lambda x, y, z, c: (x, y, z ^ 1, c),
        lambda x, y, z, c: (x, y, z ^ 2, c),
    ):
        value = value + permute(value, move)
    return value


def dot(a, b):
    return jnp.dot(a, b, preferred_element_type=F32)


def dot_t(a, b):
    return lax.dot_general(a, b, (((0,), (0,)), ((), ())), preferred_element_type=F32)


def gather_columns(block):
    arrived = {0: block}
    for j in (1, 3, 2):
        arrived[j] = from_y(block, j)
    return [jnp.concatenate([arrived[j], swap_cores(arrived[j])], axis=1) for j in range(4)]


def rows_at(value, index, size):
    return lax.dynamic_slice_in_dim(value, index * size, size, 0)


def place(blocks, first):
    size = blocks[0].shape[0]
    out = jnp.zeros((4 * size,) + blocks[0].shape[1:], blocks[0].dtype)
    for e, block in enumerate(blocks):
        out = lax.dynamic_update_slice_in_dim(out, block, ((first + e) % 4) * size, 0)
    return out


def local(unfolding):
    x_hi = lax.axis_index("xhi")
    x = 2 * x_hi + lax.axis_index("xlo")
    z = lax.axis_index("z")
    core = lax.axis_index("core")
    major = jnp.where(core == 0, x, z)
    minor = jnp.where(core == 0, z, x)

    half = unfolding.shape[0] // 2
    values = unfolding.astype(F32)
    sums = jnp.sum(sum_over_all(jnp.sum((values * values).reshape(-1, 8, 2, 128), axis=(0, 2))))
    factor = math.sqrt(COLS) / (3.0 * jnp.sqrt(sums))

    mine = lax.dynamic_slice_in_dim(unfolding, x_hi * half, half, 0)
    other = permute(
        lax.dynamic_slice_in_dim(unfolding, (1 - x_hi) * half, half, 0),
        lambda x, y, z, c: (x + 2, y, z, c),
    )
    current = jnp.concatenate(
        [jnp.where(x_hi == 0, mine, other), jnp.where(x_hi == 0, other, mine)], axis=1
    )
    scale = factor
    for turn_index in range(ITERS):
        blocks = gather_columns(current)
        whole = jnp.concatenate(blocks, axis=1)
        width = blocks[0].shape[1]
        slices = [
            lax.dynamic_slice_in_dim(whole, ((major + d) % 4) * width, width, 1) for d in range(4)
        ]
        total = dot_t(slices[0], current)
        for d in (1, 3, 2):
            total = total + to_major(dot_t(slices[d], current).astype(BF), d).astype(F32)
        piece = total.shape[0] // 4
        share = rows_at(total, minor, piece)
        for e in (1, 3, 2):
            share = share + to_minor(rows_at(total, (minor + e) % 4, piece).astype(BF), e).astype(F32)
        share = (share * (scale * scale)).astype(BF)
        quarter = place([share] + [to_minor(share, -e) for e in (1, 2, 3)], minor)
        gram = [quarter] + [to_major(quarter, -d) for d in (1, 2, 3)]
        first = dot(slices[0], gram[0])
        for d in (1, 3, 2):
            first = first + dot(slices[d], gram[d])
        first = (first * scale).astype(BF)
        ordered = place(gram, major)
        firsts = gather_columns(first)
        second = dot(firsts[0], rows_at(ordered, 0, width))
        for j in (1, 3, 2):
            second = second + dot(firsts[j], rows_at(ordered, j, width))
        updated = (
            (1.875 * scale) * current.astype(F32) - 1.25 * first.astype(F32) + 0.375 * second
        )
        current = updated.astype(BF)
        scale = jnp.float32(1.0)

    final = (updated * math.sqrt(ROWS)).astype(BF)
    pixels = final.shape[1] // 2
    parts = final.reshape(half, 2, 16, pixels // 16).transpose(2, 3, 1, 0)
    parts = lax.all_to_all(parts, ("y", "xhi", "core"), split_axis=0, concat_axis=0, tiled=True)
    parts = parts.reshape(4, 2, 2, pixels // 16, 2, half).transpose(3, 0, 4, 2, 1, 5)
    return parts.reshape(pixels // 16, 16, 2 * half)


def solution(mesh):
    wide = Mesh(mesh.devices.reshape(2, 4, 4, 2, 2), AXES)
    return jax.shard_map(
        local,
        mesh=wide,
        in_specs=(P(("xlo", "z"), ("y", "xhi", "core")),),
        out_specs=P(("y", "xhi", "core"), None, ("xlo", "z")),
        check_vma=False,
    )
```

```python
import math

import jax
import jax.numpy as jnp
from jax import lax
from jax.sharding import Mesh
from jax.sharding import PartitionSpec as P

ITERS = 2
ROWS = 6144
COLS = 4096
BF = jnp.bfloat16
F32 = jnp.float32

AXES = ("xlo", "z", "y", "xhi", "core")


def pairs(move):
    out = []
    for xlo in range(2):
        for z in range(4):
            for y in range(4):
                for xhi in range(2):
                    for c in range(2):
                        x = 2 * xhi + xlo
                        x2, y2, z2, c2 = move(x, y, z, c)
                        x2, y2, z2, c2 = x2 % 4, y2 % 4, z2 % 4, c2 % 2
                        src = (((xlo * 4 + z) * 4 + y) * 2 + xhi) * 2 + c
                        dst = ((((x2 % 2) * 4 + z2) * 4 + y2) * 2 + x2 // 2) * 2 + c2
                        out.append((src, dst))
    return out


def permute(value, move):
    return lax.ppermute(value, AXES, pairs(move))


def swap_cores(value):
    return permute(value, lambda x, y, z, c: (x, y, z, 1 - c))


def from_y(value, j):
    return permute(value, lambda x, y, z, c: (x, y - j, z, c))


def to_major(value, d):
    return permute(value, lambda x, y, z, c: (x + d, y, z, c) if c == 0 else (x, y, z + d, c))


def to_minor(value, d):
    return permute(value, lambda x, y, z, c: (x, y, z + d, c) if c == 0 else (x + d, y, z, c))


def dot(a, b):
    return jnp.dot(a, b, preferred_element_type=F32)


def dot_t(a, b):
    return lax.dot_general(a, b, (((0,), (0,)), ((), ())), preferred_element_type=F32)


def gather_columns(block):
    width = block.shape[1] // 2
    above = from_y(block, 1)
    below = from_y(block, 3)
    far = [from_y(above[:, :width], 1), from_y(below[:, width:], 3)]
    return [
        jnp.concatenate(parts + [swap_cores(part) for part in parts], axis=1)
        for parts in ([block], [above], far, [below])
    ]


def rows_at(value, index, size):
    return lax.dynamic_slice_in_dim(value, index * size, size, 0)


def place(blocks, first):
    size = blocks[0].shape[0]
    out = jnp.zeros((4 * size,) + blocks[0].shape[1:], blocks[0].dtype)
    for e, block in enumerate(blocks):
        out = lax.dynamic_update_slice_in_dim(out, block, ((first + e) % 4) * size, 0)
    return out


def local(unfolding):
    x_hi = lax.axis_index("xhi")
    x = 2 * x_hi + lax.axis_index("xlo")
    z = lax.axis_index("z")
    core = lax.axis_index("core")
    major = jnp.where(core == 0, x, z)
    minor = jnp.where(core == 0, z, x)

    half = unfolding.shape[0] // 2
    mine = lax.dynamic_slice_in_dim(unfolding, x_hi * half, half, 0)
    other = permute(
        lax.dynamic_slice_in_dim(unfolding, (1 - x_hi) * half, half, 0),
        lambda x, y, z, c: (x + 2, y, z, c),
    )
    current = jnp.concatenate(
        [jnp.where(x_hi == 0, mine, other), jnp.where(x_hi == 0, other, mine)], axis=1
    )
    current = lax.optimization_barrier(current)
    scale = None
    for turn_index in range(ITERS):
        blocks = gather_columns(current)
        whole = jnp.concatenate(blocks, axis=1)
        width = blocks[0].shape[1]
        slices = [
            lax.dynamic_slice_in_dim(whole, ((major + d) % 4) * width, width, 1) for d in range(4)
        ]
        products = [dot_t(slices[d], current) for d in (0, 1, 3, 2)]
        total = products[0]
        leaving = [product.astype(BF) for product in products[1:]]
        arriving = [to_major(value, d) for value, d in zip(leaving, (1, 3, 2))]
        if turn_index == 0:
            values = whole.astype(F32)
            tile = jnp.sum((values * values).reshape(half // 8, 8, -1, 128), axis=(0, 2))
            tile, leaving = lax.optimization_barrier((tile, leaving))
            tiles = lax.all_to_all(
                jnp.broadcast_to(tile, (16, 8, 128)), ("xlo", "z", "xhi"), 0, 0, tiled=True
            )
            scale = math.sqrt(COLS) / (3.0 * jnp.sqrt(jnp.sum(tiles)))
            arriving, scale = lax.optimization_barrier((arriving, scale))
        for value in arriving:
            total = total + value.astype(F32)
        piece = total.shape[0] // 4
        share = rows_at(total, minor, piece)
        for e in (1, 3, 2):
            share = share + to_minor(rows_at(total, (minor + e) % 4, piece).astype(BF), e).astype(F32)
        share = (share * (scale * scale)).astype(BF)
        quarter = place([share] + [to_minor(share, -e) for e in (1, 2, 3)], minor)
        above = to_major(quarter, -1)
        below = to_major(quarter, 1)
        rows = quarter.shape[0]
        far = jnp.concatenate(
            [to_major(above[: rows // 2], -1), to_major(below[rows // 2 :], 1)], axis=0
        )
        gram = [quarter, above, far, below]
        first = dot(slices[0], gram[0])
        for d in (1, 3, 2):
            first = first + dot(slices[d], gram[d])
        first = (first * scale).astype(BF)
        ordered = place(gram, major)
        firsts = gather_columns(first)
        second = dot(firsts[0], rows_at(ordered, 0, width))
        for j in (1, 3, 2):
            second = second + dot(firsts[j], rows_at(ordered, j, width))
        updated = (
            (1.875 * scale) * current.astype(F32) - 1.25 * first.astype(F32) + 0.375 * second
        )
        current = updated.astype(BF)
        scale = jnp.float32(1.0)

    final = (updated * math.sqrt(ROWS)).astype(BF)
    pixels = final.shape[1] // 2
    parts = final.reshape(half, 2, 16, pixels // 16).transpose(2, 3, 1, 0)
    parts = lax.all_to_all(parts, ("y", "xhi", "core"), split_axis=0, concat_axis=0, tiled=True)
    parts = parts.reshape(4, 2, 2, pixels // 16, 2, half).transpose(3, 0, 4, 2, 1, 5)
    return parts.reshape(pixels // 16, 16, 2 * half)


def solution(mesh):
    wide = Mesh(mesh.devices.reshape(2, 4, 4, 2, 2), AXES)
    return jax.shard_map(
        local,
        mesh=wide,
        in_specs=(P(("xlo", "z"), ("y", "xhi", "core")),),
        out_specs=P(("y", "xhi", "core"), None, ("xlo", "z")),
        check_vma=False,
    )
```

```python
import math

import jax
import jax.numpy as jnp
from jax import lax
from jax.experimental import pallas as pl
from jax.experimental.pallas import tpu as pltpu
from jax.sharding import Mesh
from jax.sharding import PartitionSpec as P

ITERS = 2
ROWS = 6144
COLS = 4096
BF = jnp.bfloat16
F32 = jnp.float32

AXES = ("xlo", "z", "y", "xhi", "core")


def pairs(move):
    out = []
    for xlo in range(2):
        for z in range(4):
            for y in range(4):
                for xhi in range(2):
                    for c in range(2):
                        x = 2 * xhi + xlo
                        x2, y2, z2, c2 = move(x, y, z, c)
                        x2, y2, z2, c2 = x2 % 4, y2 % 4, z2 % 4, c2 % 2
                        src = (((xlo * 4 + z) * 4 + y) * 2 + xhi) * 2 + c
                        dst = ((((x2 % 2) * 4 + z2) * 4 + y2) * 2 + x2 // 2) * 2 + c2
                        out.append((src, dst))
    return out


def permute(value, move):
    return lax.ppermute(value, AXES, pairs(move))


def swap_cores(value):
    return permute(value, lambda x, y, z, c: (x, y, z, 1 - c))


def from_y(value, j):
    return permute(value, lambda x, y, z, c: (x, y - j, z, c))


def to_major(value, d):
    return permute(value, lambda x, y, z, c: (x + d, y, z, c) if c == 0 else (x, y, z + d, c))


def to_minor(value, d):
    return permute(value, lambda x, y, z, c: (x, y, z + d, c) if c == 0 else (x + d, y, z, c))


def dot(a, b):
    return jnp.dot(a, b, preferred_element_type=F32)


def dot_t(a, b):
    return lax.dot_general(a, b, (((0,), (0,)), ((), ())), preferred_element_type=F32)


def next_on_ring(block):
    return from_y(block, 1), from_y(block, 3)


def gather_columns(block, near):
    width = block.shape[1] // 2
    above, below = near
    far = [from_y(above[:, :width], 1), from_y(below[:, width:], 3)]
    return [
        jnp.concatenate(parts + [swap_cores(part) for part in parts], axis=1)
        for parts in ([block], [above], far, [below])
    ]


def rows_at(value, start, size):
    return lax.dynamic_slice(value, (start, jnp.uint32(0)), (size, value.shape[1]))


def place_kernel(starts, in0, in1, in2, in3, out):
    for e, block in enumerate((in0, in1, in2, in3)):
        rows = block.shape[0]
        out[pl.ds(pl.multiple_of(starts[e], rows), rows), :] = block[...]


def place(blocks, starts):
    vmem = pl.BlockSpec(memory_space=pltpu.VMEM)
    shape = (4 * blocks[0].shape[0], blocks[0].shape[1])
    return pl.pallas_call(
        place_kernel,
        out_shape=jax.ShapeDtypeStruct(shape, blocks[0].dtype),
        in_specs=[pl.BlockSpec(memory_space=pltpu.SMEM)] + [vmem] * 4,
        out_specs=vmem,
        compiler_params=pltpu.CompilerParams(vmem_limit_bytes=12 * 2**20),
    )(starts, *blocks)


def scale_kernel(tile, out):
    total = jnp.sum(jnp.sum(tile[...], axis=1, keepdims=True), axis=0, keepdims=True)
    out[...] = jnp.broadcast_to(math.sqrt(COLS) / (3.0 * jnp.sqrt(total)), out.shape)


def scale_row(tile, width):
    vmem = pl.BlockSpec(memory_space=pltpu.VMEM)
    return pl.pallas_call(
        scale_kernel,
        out_shape=jax.ShapeDtypeStruct((1, width), F32),
        in_specs=[vmem],
        out_specs=vmem,
        compiler_params=pltpu.CompilerParams(vmem_limit_bytes=2**20),
    )(tile)


def add_pair(value, move):
    return value + permute(value, move)


def local(unfolding):
    half = unfolding.shape[0] // 2
    width = 2 * unfolding.shape[1]
    quarter_rows = 2 * width
    piece = quarter_rows // 4

    x_hi = lax.axis_index("xhi").astype(jnp.uint32)
    x = 2 * x_hi + lax.axis_index("xlo").astype(jnp.uint32)
    z = lax.axis_index("z").astype(jnp.uint32)
    core = lax.axis_index("core")
    major = jnp.where(core == 0, x, z)
    minor = jnp.where(core == 0, z, x)
    low = x_hi == 0
    at_major = [((major + d) & 3) * quarter_rows for d in range(4)]
    at_minor = [((minor + e) & 3) * piece for e in range(4)]
    my_rows, other_rows = x_hi * half, (1 - x_hi) * half
    major_starts = jnp.stack(at_major).astype(jnp.int32)
    minor_starts = jnp.stack(at_minor).astype(jnp.int32)
    unfolding, low, at_major, at_minor, major_starts, minor_starts, my_rows, other_rows = (
        lax.optimization_barrier(
            (unfolding, low, at_major, at_minor, major_starts, minor_starts, my_rows, other_rows)
        )
    )

    mine = rows_at(unfolding, my_rows, half)
    other = permute(
        rows_at(unfolding, other_rows, half), lambda x, y, z, c: (x + 2, y, z, c)
    )
    values = unfolding.astype(F32)
    tile = jnp.sum((values * values).reshape(2 * half // 8, 8, -1, 128), axis=(0, 2))
    current = jnp.concatenate(
        [jnp.where(low, mine, other), jnp.where(low, other, mine)], axis=1
    )
    current, tile = lax.optimization_barrier((current, tile))
    for turn_index in range(ITERS):
        near = next_on_ring(current)
        if turn_index == 0:
            tile = add_pair(tile, lambda x, y, z, c: (x ^ 1, y, z, c))
            tile = add_pair(tile, lambda x, y, z, c: (x ^ 2, y, z, c))
            near, tile = lax.optimization_barrier((near, tile))
            tile = add_pair(tile, lambda x, y, z, c: (x, y, z ^ 1, c))
            tile = add_pair(tile, lambda x, y, z, c: (x, y, z ^ 2, c))
        whole = jnp.concatenate(gather_columns(current, near), axis=1)
        if turn_index == 0:
            whole, tile = lax.optimization_barrier((whole, tile))
        slices = [
            lax.dynamic_slice(whole, (jnp.uint32(0), at_major[d]), (half, quarter_rows))
            for d in range(4)
        ]
        total = dot_t(slices[0], current)
        leaving = {d: dot_t(slices[d], current).astype(BF) for d in (2, 1, 3)}
        arriving = {d: to_major(leaving[d], d) for d in (2, 1, 3)}
        if turn_index == 0:
            tile, _ = lax.optimization_barrier((tile, leaving))
            tile = add_pair(tile, lambda x, y, z, c: (x, y, z, 1 - c))
            tile = add_pair(tile, lambda x, y, z, c: (x, y ^ 1, z, c))
            tile = add_pair(tile, lambda x, y, z, c: (x, y ^ 2, z, c))
            arriving, tile = lax.optimization_barrier((arriving, tile))
            scale = scale_row(tile, width)
        for d in (1, 3, 2):
            total = total + arriving[d].astype(F32)
        share = rows_at(total, at_minor[0], piece)
        for e in (1, 3, 2):
            share = share + to_minor(rows_at(total, at_minor[e], piece).astype(BF), e).astype(F32)
        if turn_index == 0:
            share = share * (scale * scale)
        share = share.astype(BF)
        quarter = place([share] + [to_minor(share, -e) for e in (1, 2, 3)], minor_starts)
        above = to_major(quarter, -1)
        below = to_major(quarter, 1)
        rows = quarter.shape[0]
        far = jnp.concatenate(
            [to_major(above[: rows // 2], -1), to_major(below[rows // 2 :], 1)], axis=0
        )
        gram = [quarter, above, far, below]
        first = dot(slices[0], gram[0])
        for d in (1, 3, 2):
            first = first + dot(slices[d], gram[d])
        if turn_index == 0:
            first = first * scale
        first = first.astype(BF)
        ordered = place(gram, major_starts)
        firsts = gather_columns(first, next_on_ring(first))
        second = 0.0
        for j in (0, 1, 3, 2):
            second = second + dot(
                firsts[j], ordered[j * quarter_rows : (j + 1) * quarter_rows]
            )
        linear = 1.875 * current.astype(F32)
        if turn_index == 0:
            linear = linear * scale
        updated = linear - 1.25 * first.astype(F32) + 0.375 * second
        current = updated.astype(BF)

    final = (updated * math.sqrt(ROWS)).astype(BF)
    pixels = final.shape[1] // 2
    parts = final.reshape(half, 2, 16, pixels // 16).transpose(2, 3, 1, 0)
    parts = lax.all_to_all(parts, ("y", "xhi", "core"), split_axis=0, concat_axis=0, tiled=True)
    parts = parts.reshape(4, 2, 2, pixels // 16, 2, half).transpose(3, 0, 4, 2, 1, 5)
    return parts.reshape(pixels // 16, 16, 2 * half)


def solution(mesh):
    wide = Mesh(mesh.devices.reshape(2, 4, 4, 2, 2), AXES)
    return jax.shard_map(
        local,
        mesh=wide,
        in_specs=(P(("xlo", "z"), ("y", "xhi", "core")),),
        out_specs=P(("y", "xhi", "core"), None, ("xlo", "z")),
        check_vma=False,
    )
```

```python
import math

import jax
import jax.numpy as jnp
from jax import lax
from jax.experimental import pallas as pl
from jax.experimental.pallas import tpu as pltpu
from jax.sharding import Mesh
from jax.sharding import PartitionSpec as P

ITERS = 2
ROWS = 6144
COLS = 4096
BF = jnp.bfloat16
F32 = jnp.float32

AXES = ("xlo", "z", "y", "xhi", "core")


def pairs(move):
    out = []
    for xlo in range(2):
        for z in range(4):
            for y in range(4):
                for xhi in range(2):
                    for c in range(2):
                        x = 2 * xhi + xlo
                        x2, y2, z2, c2 = move(x, y, z, c)
                        x2, y2, z2, c2 = x2 % 4, y2 % 4, z2 % 4, c2 % 2
                        src = (((xlo * 4 + z) * 4 + y) * 2 + xhi) * 2 + c
                        dst = ((((x2 % 2) * 4 + z2) * 4 + y2) * 2 + x2 // 2) * 2 + c2
                        out.append((src, dst))
    return out


def permute(value, move):
    return lax.ppermute(value, AXES, pairs(move))


def swap_cores(value):
    return permute(value, lambda x, y, z, c: (x, y, z, 1 - c))


def from_y(value, j):
    return permute(value, lambda x, y, z, c: (x, y - j, z, c))


def to_major(value, d):
    return permute(value, lambda x, y, z, c: (x + d, y, z, c) if c == 0 else (x, y, z + d, c))


def to_minor(value, d):
    return permute(value, lambda x, y, z, c: (x, y, z + d, c) if c == 0 else (x + d, y, z, c))


def dot(a, b):
    return jnp.dot(a, b, preferred_element_type=F32)


def dot_t(a, b):
    return lax.dot_general(a, b, (((0,), (0,)), ((), ())), preferred_element_type=F32)


def gather_ring(halves, fetch):
    first, last = halves
    above_first, below_last = fetch(first, 1), fetch(last, 3)
    above_last, below_first = fetch(last, 1), fetch(first, 3)
    far = [fetch(above_first, 1), fetch(below_last, 3)]
    return [[first, last], [above_first, above_last], far, [below_first, below_last]]


def with_other_core(ring):
    return [
        jnp.concatenate(parts + [swap_cores(part) for part in parts], axis=1) for parts in ring
    ]


def gather_columns(block):
    width = block.shape[1] // 2
    ring = gather_ring([block[:, :width], block[:, width:]], from_y)
    ring[0] = [block]
    return with_other_core(ring)


def rows_at(value, start, size):
    return lax.dynamic_slice(value, (start, jnp.uint32(0)), (size, value.shape[1]))


def place_kernel(starts, *refs):
    *blocks, out = refs
    each = len(blocks) // 4
    rows = blocks[0].shape[0]
    for i, block in enumerate(blocks):
        at = pl.multiple_of(starts[i // each] + i % each * rows, rows)
        out[pl.ds(at, rows), :] = block[...]


def place(blocks, starts):
    vmem = pl.BlockSpec(memory_space=pltpu.VMEM)
    shape = (len(blocks) * blocks[0].shape[0], blocks[0].shape[1])
    return pl.pallas_call(
        place_kernel,
        out_shape=jax.ShapeDtypeStruct(shape, blocks[0].dtype),
        in_specs=[pl.BlockSpec(memory_space=pltpu.SMEM)] + [vmem] * len(blocks),
        out_specs=vmem,
        compiler_params=pltpu.CompilerParams(vmem_limit_bytes=12 * 2**20),
    )(starts, *blocks)


def scale_kernel(tile, out):
    total = jnp.sum(jnp.sum(tile[...], axis=1, keepdims=True), axis=0, keepdims=True)
    out[...] = jnp.broadcast_to(math.sqrt(COLS) / (3.0 * jnp.sqrt(total)), out.shape)


def scale_row(tile, width):
    vmem = pl.BlockSpec(memory_space=pltpu.VMEM)
    return pl.pallas_call(
        scale_kernel,
        out_shape=jax.ShapeDtypeStruct((1, width), F32),
        in_specs=[vmem],
        out_specs=vmem,
        compiler_params=pltpu.CompilerParams(vmem_limit_bytes=2**20),
    )(tile)


def add_pair(value, move):
    return value + permute(value, move)


def local(unfolding):
    half = unfolding.shape[0] // 2
    width = 2 * unfolding.shape[1]
    quarter_rows = 2 * width
    piece = quarter_rows // 4

    x_hi = lax.axis_index("xhi").astype(jnp.uint32)
    x = 2 * x_hi + lax.axis_index("xlo").astype(jnp.uint32)
    z = lax.axis_index("z").astype(jnp.uint32)
    core = lax.axis_index("core")
    major = jnp.where(core == 0, x, z)
    minor = jnp.where(core == 0, z, x)
    low = x_hi == 0
    at_major = [((major + d) & 3) * quarter_rows for d in range(4)]
    at_half = [[start, start + quarter_rows // 2] for start in at_major]
    at_minor = [((minor + e) & 3) * piece for e in range(4)]
    my_rows, other_rows = x_hi * half, (1 - x_hi) * half
    major_starts = jnp.stack(at_major).astype(jnp.int32)
    minor_starts = jnp.stack(at_minor).astype(jnp.int32)
    unfolding, low, at_major, at_half, at_minor, major_starts, minor_starts, my_rows, other_rows = (
        lax.optimization_barrier(
            (unfolding, low, at_major, at_half, at_minor, major_starts, minor_starts, my_rows, other_rows)
        )
    )

    mine = rows_at(unfolding, my_rows, half)
    other = permute(
        rows_at(unfolding, other_rows, half), lambda x, y, z, c: (x + 2, y, z, c)
    )
    values = unfolding.astype(F32)
    tile = jnp.sum((values * values).reshape(2 * half // 8, 8, -1, 128), axis=(0, 2))
    current = jnp.concatenate(
        [jnp.where(low, mine, other), jnp.where(low, other, mine)], axis=1
    )
    current, tile = lax.optimization_barrier((current, tile))
    for turn_index in range(ITERS):
        if turn_index == 0:
            tile = add_pair(tile, lambda x, y, z, c: (x ^ 1, y, z, c))
            tile = add_pair(tile, lambda x, y, z, c: (x ^ 2, y, z, c))
            near = [from_y(current, 1), from_y(current, 3)]
            near, tile = lax.optimization_barrier((near, tile))
            tile = add_pair(tile, lambda x, y, z, c: (x, y, z ^ 1, c))
            tile = add_pair(tile, lambda x, y, z, c: (x, y, z ^ 2, c))
            above, below = near
            middle = current.shape[1] // 2
            far = [from_y(above[:, :middle], 1), from_y(below[:, middle:], 3)]
            whole = jnp.concatenate(with_other_core([[current], [above], far, [below]]), axis=1)
            whole, tile = lax.optimization_barrier((whole, tile))
        else:
            whole = jnp.concatenate(gather_columns(current), axis=1)
        rows = quarter_rows // 2
        halves = [
            [lax.dynamic_slice(whole, (jnp.uint32(0), start), (half, rows)) for start in starts]
            for starts in at_half
        ]

        def product(d, i):
            return dot_t(halves[d][i], current)

        pass_up = to_major(product(2, 0).astype(BF), 1)
        pass_down = to_major(product(2, 1).astype(BF), 3)
        up_last = to_major(product(1, 1).astype(BF), 1)
        down_first = to_major(product(3, 0).astype(BF), 3)
        if turn_index == 0:
            tile, _ = lax.optimization_barrier((tile, whole))
            tile = add_pair(tile, lambda x, y, z, c: (x, y, z, 1 - c))
            tile = add_pair(tile, lambda x, y, z, c: (x, y ^ 1, z, c))
            tile = add_pair(tile, lambda x, y, z, c: (x, y ^ 2, z, c))
        up_first = to_major((product(1, 0) + pass_up.astype(F32)).astype(BF), 1)
        down_last = to_major((product(3, 1) + pass_down.astype(F32)).astype(BF), 3)
        if turn_index == 0:
            up_first, down_last, tile = lax.optimization_barrier((up_first, down_last, tile))
            scale = scale_row(tile, width)
        total = jnp.concatenate(
            [
                product(0, 0) + up_first.astype(F32) + down_first.astype(F32),
                product(0, 1) + up_last.astype(F32) + down_last.astype(F32),
            ],
            axis=0,
        )
        share = rows_at(total, at_minor[0], piece)
        for e in (1, 3, 2):
            share = share + to_minor(rows_at(total, at_minor[e], piece).astype(BF), e).astype(F32)
        if turn_index == 0:
            share = share * (scale * scale)
        share = share.astype(BF)
        quarter = place([share] + [to_minor(share, -e) for e in (1, 2, 3)], minor_starts)
        gram = gather_ring([quarter[:rows], quarter[rows:]], lambda value, d: to_major(value, -d))
        first = 0.0
        for d in (0, 1, 3, 2):
            for i in range(2):
                first = first + dot(halves[d][i], gram[d][i])
        if turn_index == 0:
            first = first * scale
        first = first.astype(BF)
        ordered = place([part for parts in gram for part in parts], major_starts)
        firsts = gather_columns(first)
        second = 0.0
        for j in (0, 1, 3, 2):
            second = second + dot(
                firsts[j], ordered[j * quarter_rows : (j + 1) * quarter_rows]
            )
        linear = 1.875 * current.astype(F32)
        if turn_index == 0:
            linear = linear * scale
        updated = linear - 1.25 * first.astype(F32) + 0.375 * second
        current = updated.astype(BF)

    final = (updated * math.sqrt(ROWS)).astype(BF)
    pixels = final.shape[1] // 2
    parts = final.reshape(half, 2, 16, pixels // 16).transpose(2, 3, 1, 0)
    parts = lax.all_to_all(parts, ("y", "xhi", "core"), split_axis=0, concat_axis=0, tiled=True)
    parts = parts.reshape(4, 2, 2, pixels // 16, 2, half).transpose(3, 0, 4, 2, 1, 5)
    return parts.reshape(pixels // 16, 16, 2 * half)


def solution(mesh):
    wide = Mesh(mesh.devices.reshape(2, 4, 4, 2, 2), AXES)
    return jax.shard_map(
        local,
        mesh=wide,
        in_specs=(P(("xlo", "z"), ("y", "xhi", "core")),),
        out_specs=P(("y", "xhi", "core"), None, ("xlo", "z")),
        check_vma=False,
    )
```

```python
import math

import jax
import jax.numpy as jnp
from jax import lax
from jax.experimental import pallas as pl
from jax.experimental.pallas import tpu as pltpu
from jax.sharding import Mesh
from jax.sharding import PartitionSpec as P

ITERS = 2
ROWS = 6144
COLS = 4096
BF = jnp.bfloat16
F32 = jnp.float32

AXES = ("xlo", "z", "y", "xhi", "core")


def pairs(move):
    out = []
    for xlo in range(2):
        for z in range(4):
            for y in range(4):
                for xhi in range(2):
                    for c in range(2):
                        x = 2 * xhi + xlo
                        x2, y2, z2, c2 = move(x, y, z, c)
                        x2, y2, z2, c2 = x2 % 4, y2 % 4, z2 % 4, c2 % 2
                        src = (((xlo * 4 + z) * 4 + y) * 2 + xhi) * 2 + c
                        dst = ((((x2 % 2) * 4 + z2) * 4 + y2) * 2 + x2 // 2) * 2 + c2
                        out.append((src, dst))
    return out


def permute(value, move):
    return lax.ppermute(value, AXES, pairs(move))


def swap_cores(value):
    return permute(value, lambda x, y, z, c: (x, y, z, 1 - c))


def from_y(value, j):
    return permute(value, lambda x, y, z, c: (x, y - j, z, c))


def to_major(value, d):
    return permute(value, lambda x, y, z, c: (x + d, y, z, c) if c == 0 else (x, y, z + d, c))


def to_minor(value, d):
    return permute(value, lambda x, y, z, c: (x, y, z + d, c) if c == 0 else (x + d, y, z, c))


def dot(a, b):
    return jnp.dot(a, b, preferred_element_type=F32)


def dot_t(a, b):
    return lax.dot_general(a, b, (((0,), (0,)), ((), ())), preferred_element_type=F32)


def gather_ring(halves, fetch):
    first, last = halves
    above_first, below_last = fetch(first, 1), fetch(last, 3)
    above_last, below_first = fetch(last, 1), fetch(first, 3)
    far = [fetch(above_first, 1), fetch(below_last, 3)]
    return [[first, last], [above_first, above_last], far, [below_first, below_last]]


def with_other_core(ring):
    return [
        jnp.concatenate(parts + [swap_cores(part) for part in parts], axis=1) for parts in ring
    ]


def gather_columns(block):
    width = block.shape[1] // 2
    ring = gather_ring([block[:, :width], block[:, width:]], from_y)
    far, above_last, below_first = lax.optimization_barrier((ring[2], ring[1][1], ring[3][0]))
    return with_other_core(
        [[block], [ring[1][0], above_last], far, [below_first, ring[3][1]]]
    )


def rows_at(value, start, size):
    return lax.dynamic_slice(value, (start, jnp.uint32(0)), (size, value.shape[1]))


def place_kernel(starts, *refs):
    *blocks, out = refs
    each = len(blocks) // 4
    rows = blocks[0].shape[0]
    for i, block in enumerate(blocks):
        at = pl.multiple_of(starts[i // each] + i % each * rows, rows)
        out[pl.ds(at, rows), :] = block[...]


def place(blocks, starts):
    vmem = pl.BlockSpec(memory_space=pltpu.VMEM)
    shape = (len(blocks) * blocks[0].shape[0], blocks[0].shape[1])
    return pl.pallas_call(
        place_kernel,
        out_shape=jax.ShapeDtypeStruct(shape, blocks[0].dtype),
        in_specs=[pl.BlockSpec(memory_space=pltpu.SMEM)] + [vmem] * len(blocks),
        out_specs=vmem,
        compiler_params=pltpu.CompilerParams(vmem_limit_bytes=12 * 2**20),
    )(starts, *blocks)


def scale_kernel(tile, out):
    total = jnp.sum(jnp.sum(tile[...], axis=1, keepdims=True), axis=0, keepdims=True)
    out[...] = jnp.broadcast_to(math.sqrt(COLS) / (3.0 * jnp.sqrt(total)), out.shape)


def scale_row(tile, width):
    vmem = pl.BlockSpec(memory_space=pltpu.VMEM)
    return pl.pallas_call(
        scale_kernel,
        out_shape=jax.ShapeDtypeStruct((1, width), F32),
        in_specs=[vmem],
        out_specs=vmem,
        compiler_params=pltpu.CompilerParams(vmem_limit_bytes=2**20),
    )(tile)


def add_pair(value, move):
    return value + permute(value, move)


def local(unfolding):
    half = unfolding.shape[0] // 2
    width = 2 * unfolding.shape[1]
    quarter_rows = 2 * width
    piece = quarter_rows // 4

    x_hi = lax.axis_index("xhi").astype(jnp.uint32)
    x = 2 * x_hi + lax.axis_index("xlo").astype(jnp.uint32)
    z = lax.axis_index("z").astype(jnp.uint32)
    core = lax.axis_index("core")
    major = jnp.where(core == 0, x, z)
    minor = jnp.where(core == 0, z, x)
    low = x_hi == 0
    at_major = [((major + d) & 3) * quarter_rows for d in range(4)]
    at_half = [[start, start + quarter_rows // 2] for start in at_major]
    at_minor = [((minor + e) & 3) * piece for e in range(4)]
    my_rows, other_rows = x_hi * half, (1 - x_hi) * half
    major_starts = jnp.stack(at_major).astype(jnp.int32)
    minor_starts = jnp.stack(at_minor).astype(jnp.int32)
    unfolding, low, at_major, at_half, at_minor, major_starts, minor_starts, my_rows, other_rows = (
        lax.optimization_barrier(
            (unfolding, low, at_major, at_half, at_minor, major_starts, minor_starts, my_rows, other_rows)
        )
    )

    mine = rows_at(unfolding, my_rows, half)
    other = permute(
        rows_at(unfolding, other_rows, half), lambda x, y, z, c: (x + 2, y, z, c)
    )
    values = unfolding.astype(F32)
    tile = jnp.sum((values * values).reshape(2 * half // 8, 8, -1, 128), axis=(0, 2))
    current = jnp.concatenate(
        [jnp.where(low, mine, other), jnp.where(low, other, mine)], axis=1
    )
    current, tile = lax.optimization_barrier((current, tile))
    for turn_index in range(ITERS):
        if turn_index == 0:
            tile = add_pair(tile, lambda x, y, z, c: (x ^ 1, y, z, c))
            tile = add_pair(tile, lambda x, y, z, c: (x ^ 2, y, z, c))
            near = [from_y(current, 1), from_y(current, 3)]
            near, tile = lax.optimization_barrier((near, tile))
            tile = add_pair(tile, lambda x, y, z, c: (x, y, z ^ 1, c))
            tile = add_pair(tile, lambda x, y, z, c: (x, y, z ^ 2, c))
            above, below = near
            middle = current.shape[1] // 2
            far = [from_y(above[:, :middle], 1), from_y(below[:, middle:], 3)]
            whole = jnp.concatenate(with_other_core([[current], [above], far, [below]]), axis=1)
            whole, tile = lax.optimization_barrier((whole, tile))
        else:
            whole = jnp.concatenate(gather_columns(current), axis=1)
        rows = quarter_rows // 2
        halves = [
            [lax.dynamic_slice(whole, (jnp.uint32(0), start), (half, rows)) for start in starts]
            for starts in at_half
        ]

        def product(d, i):
            return dot_t(halves[d][i], current)

        pass_up = to_major(product(2, 0).astype(BF), 1)
        pass_down = to_major(product(2, 1).astype(BF), 3)
        down_first = to_major(product(3, 0).astype(BF), 3)
        up_last = to_major(product(1, 1).astype(BF), 1)
        if turn_index == 0:
            tile, _ = lax.optimization_barrier((tile, whole))
            tile = add_pair(tile, lambda x, y, z, c: (x, y, z, 1 - c))
            tile = add_pair(tile, lambda x, y, z, c: (x, y ^ 1, z, c))
            tile = add_pair(tile, lambda x, y, z, c: (x, y ^ 2, z, c))
        up_first = to_major((product(1, 0) + pass_up.astype(F32)).astype(BF), 1)
        down_last = to_major((product(3, 1) + pass_down.astype(F32)).astype(BF), 3)
        if turn_index == 0:
            up_first, down_last, tile = lax.optimization_barrier((up_first, down_last, tile))
            scale = scale_row(tile, width)
        up_first, down_last, up_last, down_first = lax.optimization_barrier(
            (up_first, down_last, up_last, down_first)
        )
        total = jnp.concatenate(
            [
                product(0, 0) + up_first.astype(F32) + down_first.astype(F32),
                product(0, 1) + up_last.astype(F32) + down_last.astype(F32),
            ],
            axis=0,
        )
        share = rows_at(total, at_minor[0], piece)
        for e in (1, 3, 2):
            share = share + to_minor(rows_at(total, at_minor[e], piece).astype(BF), e).astype(F32)
        if turn_index == 0:
            share = share * (scale * scale)
        share = share.astype(BF)
        quarter = place([share] + [to_minor(share, -e) for e in (1, 2, 3)], minor_starts)
        gram = gather_ring([quarter[:rows], quarter[rows:]], lambda value, d: to_major(value, -d))
        first = 0.0
        for d in (0, 1, 3, 2):
            for i in range(2):
                first = first + dot(halves[d][i], gram[d][i])
        if turn_index == 0:
            first = first * scale
        first = first.astype(BF)
        ordered = place([part for parts in gram for part in parts], major_starts)
        firsts = gather_columns(first)
        second = 0.0
        for j in (0, 1, 3, 2):
            second = second + dot(
                firsts[j], ordered[j * quarter_rows : (j + 1) * quarter_rows]
            )
        linear = 1.875 * current.astype(F32)
        if turn_index == 0:
            linear = linear * scale
        updated = linear - 1.25 * first.astype(F32) + 0.375 * second
        current = updated.astype(BF)

    final = (updated * math.sqrt(ROWS)).astype(BF)
    pixels = final.shape[1] // 2
    parts = final.reshape(half, 2, 16, pixels // 16).transpose(2, 3, 1, 0)
    parts = lax.all_to_all(parts, ("y", "xhi", "core"), split_axis=0, concat_axis=0, tiled=True)
    parts = parts.reshape(4, 2, 2, pixels // 16, 2, half).transpose(3, 0, 4, 2, 1, 5)
    return parts.reshape(pixels // 16, 16, 2 * half)


def solution(mesh):
    wide = Mesh(mesh.devices.reshape(2, 4, 4, 2, 2), AXES)
    return jax.shard_map(
        local,
        mesh=wide,
        in_specs=(P(("xlo", "z"), ("y", "xhi", "core")),),
        out_specs=P(("y", "xhi", "core"), None, ("xlo", "z")),
        check_vma=False,
    )
```

```python
import math

import jax
import jax.numpy as jnp
from jax import lax
from jax.experimental import pallas as pl
from jax.experimental.pallas import tpu as pltpu
from jax.sharding import Mesh
from jax.sharding import PartitionSpec as P

ITERS = 2
ROWS = 6144
COLS = 4096
BF = jnp.bfloat16
F32 = jnp.float32

AXES = ("xlo", "z", "y", "xhi", "core")


def pairs(move):
    out = []
    for xlo in range(2):
        for z in range(4):
            for y in range(4):
                for xhi in range(2):
                    for c in range(2):
                        x = 2 * xhi + xlo
                        x2, y2, z2, c2 = move(x, y, z, c)
                        x2, y2, z2, c2 = x2 % 4, y2 % 4, z2 % 4, c2 % 2
                        src = (((xlo * 4 + z) * 4 + y) * 2 + xhi) * 2 + c
                        dst = ((((x2 % 2) * 4 + z2) * 4 + y2) * 2 + x2 // 2) * 2 + c2
                        out.append((src, dst))
    return out


def permute(value, move):
    return lax.ppermute(value, AXES, pairs(move))


def swap_cores(value):
    return permute(value, lambda x, y, z, c: (x, y, z, 1 - c))


def from_y(value, j):
    return permute(value, lambda x, y, z, c: (x, y - j, z, c))


def to_major(value, d):
    return permute(value, lambda x, y, z, c: (x + d, y, z, c) if c == 0 else (x, y, z + d, c))


def to_minor(value, d):
    return permute(value, lambda x, y, z, c: (x, y, z + d, c) if c == 0 else (x + d, y, z, c))


def dot(a, b):
    return jnp.dot(a, b, preferred_element_type=F32)


def dot_t(a, b):
    return lax.dot_general(a, b, (((0,), (0,)), ((), ())), preferred_element_type=F32)


def gather_ring(halves, fetch):
    first, last = halves
    above_first, below_last = fetch(first, 1), fetch(last, 3)
    above_last, below_first = fetch(last, 1), fetch(first, 3)
    far = [fetch(above_first, 1), fetch(below_last, 3)]
    return [[first, last], [above_first, above_last], far, [below_first, below_last]]


def with_other_core(ring):
    return [
        jnp.concatenate(parts + [swap_cores(part) for part in parts], axis=1) for parts in ring
    ]


def gather_columns(block):
    width = block.shape[1] // 2
    ring = gather_ring([block[:, :width], block[:, width:]], from_y)
    far, above_last, below_first = lax.optimization_barrier((ring[2], ring[1][1], ring[3][0]))
    return with_other_core(
        [[block], [ring[1][0], above_last], far, [below_first, ring[3][1]]]
    )


def rows_at(value, start, size):
    return lax.dynamic_slice(value, (start, jnp.uint32(0)), (size, value.shape[1]))


def place_kernel(starts, *refs):
    *blocks, out = refs
    each = len(blocks) // 4
    rows = blocks[0].shape[0]
    for i, block in enumerate(blocks):
        at = pl.multiple_of(starts[i // each] + i % each * rows, rows)
        out[pl.ds(at, rows), :] = block[...]


def place(blocks, starts):
    vmem = pl.BlockSpec(memory_space=pltpu.VMEM)
    shape = (len(blocks) * blocks[0].shape[0], blocks[0].shape[1])
    return pl.pallas_call(
        place_kernel,
        out_shape=jax.ShapeDtypeStruct(shape, blocks[0].dtype),
        in_specs=[pl.BlockSpec(memory_space=pltpu.SMEM)] + [vmem] * len(blocks),
        out_specs=vmem,
        compiler_params=pltpu.CompilerParams(vmem_limit_bytes=12 * 2**20),
    )(starts, *blocks)


def scale_kernel(tile, out):
    total = jnp.sum(jnp.sum(tile[...], axis=1, keepdims=True), axis=0, keepdims=True)
    out[...] = jnp.broadcast_to(math.sqrt(COLS) / (3.0 * jnp.sqrt(total)), out.shape)


def scale_row(tile, width):
    vmem = pl.BlockSpec(memory_space=pltpu.VMEM)
    return pl.pallas_call(
        scale_kernel,
        out_shape=jax.ShapeDtypeStruct((1, width), F32),
        in_specs=[vmem],
        out_specs=vmem,
        compiler_params=pltpu.CompilerParams(vmem_limit_bytes=2**20),
    )(tile)


def add_pair(value, move):
    return value + permute(value, move)


def local(unfolding):
    half = unfolding.shape[0] // 2
    width = 2 * unfolding.shape[1]
    quarter_rows = 2 * width
    piece = quarter_rows // 4

    x_hi = lax.axis_index("xhi").astype(jnp.uint32)
    x = 2 * x_hi + lax.axis_index("xlo").astype(jnp.uint32)
    z = lax.axis_index("z").astype(jnp.uint32)
    core = lax.axis_index("core")
    major = jnp.where(core == 0, x, z)
    minor = jnp.where(core == 0, z, x)
    low = x_hi == 0
    at_major = [((major + d) & 3) * quarter_rows for d in range(4)]
    at_half = [[start, start + quarter_rows // 2] for start in at_major]
    at_minor = [((minor + e) & 3) * piece for e in range(4)]
    my_rows, other_rows = x_hi * half, (1 - x_hi) * half
    major_starts = jnp.stack(at_major).astype(jnp.int32)
    minor_starts = jnp.stack(at_minor).astype(jnp.int32)
    unfolding, low, at_major, at_half, at_minor, major_starts, minor_starts, my_rows, other_rows = (
        lax.optimization_barrier(
            (unfolding, low, at_major, at_half, at_minor, major_starts, minor_starts, my_rows, other_rows)
        )
    )

    mine = rows_at(unfolding, my_rows, half)
    other = permute(
        rows_at(unfolding, other_rows, half), lambda x, y, z, c: (x + 2, y, z, c)
    )
    values = unfolding.astype(F32)
    tile = jnp.sum((values * values).reshape(2 * half // 8, 8, -1, 128), axis=(0, 2))
    tile = add_pair(tile, lambda x, y, z, c: (x, y, z ^ 1, c))
    other, tile = lax.optimization_barrier((other, tile))
    current = jnp.concatenate(
        [jnp.where(low, mine, other), jnp.where(low, other, mine)], axis=1
    )
    current, tile = lax.optimization_barrier((current, tile))
    for turn_index in range(ITERS):
        if turn_index == 0:
            tile = add_pair(tile, lambda x, y, z, c: (x ^ 1, y, z, c))
            tile = add_pair(tile, lambda x, y, z, c: (x ^ 2, y, z, c))
            near = [from_y(current, 1), from_y(current, 3)]
            near, tile = lax.optimization_barrier((near, tile))
            tile = add_pair(tile, lambda x, y, z, c: (x, y, z ^ 2, c))
            above, below = near
            middle = current.shape[1] // 2
            far = [from_y(above[:, :middle], 1), from_y(below[:, middle:], 3)]
            whole = jnp.concatenate(with_other_core([[current], [above], far, [below]]), axis=1)
            whole, tile = lax.optimization_barrier((whole, tile))
        else:
            whole = jnp.concatenate(gather_columns(current), axis=1)
        rows = quarter_rows // 2
        halves = [
            [lax.dynamic_slice(whole, (jnp.uint32(0), start), (half, rows)) for start in starts]
            for starts in at_half
        ]

        def product(d, i):
            return dot_t(halves[d][i], current)

        pass_up = to_major(product(2, 0).astype(BF), 1)
        pass_down = to_major(product(2, 1).astype(BF), 3)
        down_first = to_major(product(3, 0).astype(BF), 3)
        up_last = to_major(product(1, 1).astype(BF), 1)
        if turn_index == 0:
            tile, _ = lax.optimization_barrier((tile, whole))
            tile = add_pair(tile, lambda x, y, z, c: (x, y, z, 1 - c))
            tile = add_pair(tile, lambda x, y, z, c: (x, y ^ 1, z, c))
            tile = add_pair(tile, lambda x, y, z, c: (x, y ^ 2, z, c))
        up_first = to_major((product(1, 0) + pass_up.astype(F32)).astype(BF), 1)
        down_last = to_major((product(3, 1) + pass_down.astype(F32)).astype(BF), 3)
        if turn_index == 0:
            up_first, down_last, tile = lax.optimization_barrier((up_first, down_last, tile))
            scale = scale_row(tile, width)
        up_first, down_last, up_last, down_first = lax.optimization_barrier(
            (up_first, down_last, up_last, down_first)
        )
        total = jnp.concatenate(
            [
                product(0, 0) + up_first.astype(F32) + down_first.astype(F32),
                product(0, 1) + up_last.astype(F32) + down_last.astype(F32),
            ],
            axis=0,
        )
        share = rows_at(total, at_minor[0], piece)
        for e in (1, 3, 2):
            share = share + to_minor(rows_at(total, at_minor[e], piece).astype(BF), e).astype(F32)
        if turn_index == 0:
            share = share * (scale * scale)
        share = share.astype(BF)
        quarter = place([share] + [to_minor(share, -e) for e in (1, 2, 3)], minor_starts)
        gram = gather_ring([quarter[:rows], quarter[rows:]], lambda value, d: to_major(value, -d))
        first = 0.0
        for d in (0, 1, 3, 2):
            for i in range(2):
                first = first + dot(halves[d][i], gram[d][i])
        if turn_index == 0:
            first = first * scale
        first = first.astype(BF)
        ordered = place([part for parts in gram for part in parts], major_starts)
        firsts = gather_columns(first)
        second = 0.0
        for j in (0, 1, 3, 2):
            second = second + dot(
                firsts[j], ordered[j * quarter_rows : (j + 1) * quarter_rows]
            )
        linear = 1.875 * current.astype(F32)
        if turn_index == 0:
            linear = linear * scale
        updated = linear - 1.25 * first.astype(F32) + 0.375 * second
        current = updated.astype(BF)

    final = (updated * math.sqrt(ROWS)).astype(BF)
    pixels = final.shape[1] // 2
    parts = final.reshape(half, 2, 16, pixels // 16).transpose(2, 3, 1, 0)
    parts = lax.all_to_all(parts, ("y", "xhi", "core"), split_axis=0, concat_axis=0, tiled=True)
    parts = parts.reshape(4, 2, 2, pixels // 16, 2, half).transpose(3, 0, 4, 2, 1, 5)
    return parts.reshape(pixels // 16, 16, 2 * half)


def solution(mesh):
    wide = Mesh(mesh.devices.reshape(2, 4, 4, 2, 2), AXES)
    return jax.shard_map(
        local,
        mesh=wide,
        in_specs=(P(("xlo", "z"), ("y", "xhi", "core")),),
        out_specs=P(("y", "xhi", "core"), None, ("xlo", "z")),
        check_vma=False,
    )
```

```python
import math

import jax
import jax.numpy as jnp
from jax import lax
from jax.experimental import pallas as pl
from jax.experimental.pallas import tpu as pltpu
from jax.sharding import Mesh
from jax.sharding import PartitionSpec as P

ITERS = 2
ROWS = 6144
COLS = 4096
BF = jnp.bfloat16
F32 = jnp.float32

AXES = ("xlo", "z", "y", "xhi", "core")


def pairs(move):
    out = []
    for xlo in range(2):
        for z in range(4):
            for y in range(4):
                for xhi in range(2):
                    for c in range(2):
                        x = 2 * xhi + xlo
                        x2, y2, z2, c2 = move(x, y, z, c)
                        x2, y2, z2, c2 = x2 % 4, y2 % 4, z2 % 4, c2 % 2
                        src = (((xlo * 4 + z) * 4 + y) * 2 + xhi) * 2 + c
                        dst = ((((x2 % 2) * 4 + z2) * 4 + y2) * 2 + x2 // 2) * 2 + c2
                        out.append((src, dst))
    return out


def permute(value, move):
    return lax.ppermute(value, AXES, pairs(move))


def swap_cores(value):
    return permute(value, lambda x, y, z, c: (x, y, z, 1 - c))


def from_y(value, j):
    return permute(value, lambda x, y, z, c: (x, y - j, z, c))


def to_major(value, d):
    return permute(value, lambda x, y, z, c: (x + d, y, z, c) if c == 0 else (x, y, z + d, c))


def to_minor(value, d):
    return permute(value, lambda x, y, z, c: (x, y, z + d, c) if c == 0 else (x + d, y, z, c))


def dot(a, b):
    return jnp.dot(a, b, preferred_element_type=F32)


def dot_t(a, b):
    return lax.dot_general(a, b, (((0,), (0,)), ((), ())), preferred_element_type=F32)


def gather_ring(halves, fetch):
    first, last = halves
    above_first, below_last = fetch(first, 1), fetch(last, 3)
    above_last, below_first = fetch(last, 1), fetch(first, 3)
    far = [fetch(above_first, 1), fetch(below_last, 3)]
    return [[first, last], [above_first, above_last], far, [below_first, below_last]]


def with_other_core(ring):
    return [
        jnp.concatenate(parts + [swap_cores(part) for part in parts], axis=1) for parts in ring
    ]


def gather_columns(block):
    width = block.shape[1] // 2
    ring = gather_ring([block[:, :width], block[:, width:]], from_y)
    far, above_last, below_first = lax.optimization_barrier((ring[2], ring[1][1], ring[3][0]))
    return with_other_core(
        [[block], [ring[1][0], above_last], far, [below_first, ring[3][1]]]
    )


def rows_at(value, start, size):
    return lax.dynamic_slice(value, (start, jnp.uint32(0)), (size, value.shape[1]))


def place_kernel(starts, *refs):
    *blocks, out = refs
    each = len(blocks) // 4
    rows = blocks[0].shape[0]
    for i, block in enumerate(blocks):
        at = pl.multiple_of(starts[i // each] + i % each * rows, rows)
        out[pl.ds(at, rows), :] = block[...]


def place(blocks, starts):
    vmem = pl.BlockSpec(memory_space=pltpu.VMEM)
    shape = (len(blocks) * blocks[0].shape[0], blocks[0].shape[1])
    return pl.pallas_call(
        place_kernel,
        out_shape=jax.ShapeDtypeStruct(shape, blocks[0].dtype),
        in_specs=[pl.BlockSpec(memory_space=pltpu.SMEM)] + [vmem] * len(blocks),
        out_specs=vmem,
        compiler_params=pltpu.CompilerParams(vmem_limit_bytes=12 * 2**20),
    )(starts, *blocks)


def scale_kernel(tile, out):
    total = jnp.sum(jnp.sum(tile[...], axis=1, keepdims=True), axis=0, keepdims=True)
    out[...] = jnp.broadcast_to(math.sqrt(COLS) / (3.0 * jnp.sqrt(total)), out.shape)


def scale_row(tile, width):
    vmem = pl.BlockSpec(memory_space=pltpu.VMEM)
    return pl.pallas_call(
        scale_kernel,
        out_shape=jax.ShapeDtypeStruct((1, width), F32),
        in_specs=[vmem],
        out_specs=vmem,
        compiler_params=pltpu.CompilerParams(vmem_limit_bytes=2**20),
    )(tile)


def add_pair(value, move):
    return value + permute(value, move)


def local(unfolding):
    half = unfolding.shape[0] // 2
    width = 2 * unfolding.shape[1]
    quarter_rows = 2 * width
    piece = quarter_rows // 4

    x_hi = lax.axis_index("xhi").astype(jnp.uint32)
    x = 2 * x_hi + lax.axis_index("xlo").astype(jnp.uint32)
    z = lax.axis_index("z").astype(jnp.uint32)
    core = lax.axis_index("core")
    major = jnp.where(core == 0, x, z)
    minor = jnp.where(core == 0, z, x)
    low = x_hi == 0
    at_major = [((major + d) & 3) * quarter_rows for d in range(4)]
    at_half = [[start, start + quarter_rows // 2] for start in at_major]
    at_minor = [((minor + e) & 3) * piece for e in range(4)]
    my_rows, other_rows = x_hi * half, (1 - x_hi) * half
    major_starts = jnp.stack(at_major).astype(jnp.int32)
    minor_starts = jnp.stack(at_minor).astype(jnp.int32)
    unfolding, low, at_major, at_half, at_minor, major_starts, minor_starts, my_rows, other_rows = (
        lax.optimization_barrier(
            (unfolding, low, at_major, at_half, at_minor, major_starts, minor_starts, my_rows, other_rows)
        )
    )

    mine = rows_at(unfolding, my_rows, half)
    other = permute(
        rows_at(unfolding, other_rows, half), lambda x, y, z, c: (x + 2, y, z, c)
    )
    values = unfolding.astype(F32)
    tile = jnp.sum((values * values).reshape(2 * half // 8, 8, -1, 128), axis=(0, 2))
    tile = add_pair(tile, lambda x, y, z, c: (x, y, z ^ 1, c))
    other, tile = lax.optimization_barrier((other, tile))
    current = jnp.concatenate(
        [jnp.where(low, mine, other), jnp.where(low, other, mine)], axis=1
    )
    current, tile = lax.optimization_barrier((current, tile))
    for turn_index in range(ITERS):
        if turn_index == 0:
            tile = add_pair(tile, lambda x, y, z, c: (x ^ 1, y, z, c))
            tile = add_pair(tile, lambda x, y, z, c: (x ^ 2, y, z, c))
            near = [from_y(current, 1), from_y(current, 3)]
            near, tile = lax.optimization_barrier((near, tile))
            tile = add_pair(tile, lambda x, y, z, c: (x, y, z ^ 2, c))
            above, below = near
            middle = current.shape[1] // 2
            far = [from_y(above[:, :middle], 1), from_y(below[:, middle:], 3)]
            whole = jnp.concatenate(with_other_core([[current], [above], far, [below]]), axis=1)
            whole, tile = lax.optimization_barrier((whole, tile))
        else:
            whole = jnp.concatenate(gather_columns(current), axis=1)
        rows = quarter_rows // 2
        halves = [
            [lax.dynamic_slice(whole, (jnp.uint32(0), start), (half, rows)) for start in starts]
            for starts in at_half
        ]

        def product(d, i):
            return dot_t(halves[d][i], current)

        pass_up = to_major(product(2, 0).astype(BF), 1)
        pass_down = to_major(product(2, 1).astype(BF), 3)
        down_first = to_major(product(3, 0).astype(BF), 3)
        up_last = to_major(product(1, 1).astype(BF), 1)
        if turn_index == 0:
            tile, _ = lax.optimization_barrier((tile, whole))
            tile = add_pair(tile, lambda x, y, z, c: (x, y, z, 1 - c))
            tile = add_pair(tile, lambda x, y, z, c: (x, y ^ 1, z, c))
            tile = add_pair(tile, lambda x, y, z, c: (x, y ^ 2, z, c))
        up_first = to_major((product(1, 0) + pass_up.astype(F32)).astype(BF), 1)
        down_last = to_major((product(3, 1) + pass_down.astype(F32)).astype(BF), 3)
        if turn_index == 0:
            up_first, down_last, tile = lax.optimization_barrier((up_first, down_last, tile))
            scale = scale_row(tile, width)
        own = product(0, 0), product(0, 1)
        up_first, down_last, up_last, down_first, own = lax.optimization_barrier(
            (up_first, down_last, up_last, down_first, own)
        )
        total = jnp.concatenate(
            [
                own[0] + up_first.astype(F32) + down_first.astype(F32),
                own[1] + up_last.astype(F32) + down_last.astype(F32),
            ],
            axis=0,
        )
        share = rows_at(total, at_minor[0], piece)
        for e in (1, 3, 2):
            share = share + to_minor(rows_at(total, at_minor[e], piece).astype(BF), e).astype(F32)
        if turn_index == 0:
            share = share * (scale * scale)
        share = share.astype(BF)
        quarter = place([share] + [to_minor(share, -e) for e in (1, 2, 3)], minor_starts)
        gram = gather_ring([quarter[:rows], quarter[rows:]], lambda value, d: to_major(value, -d))
        first = 0.0
        for d in (0, 1, 3, 2):
            for i in range(2):
                first = first + dot(halves[d][i], gram[d][i])
        if turn_index == 0:
            first = first * scale
        first = first.astype(BF)
        ordered = place([part for parts in gram for part in parts], major_starts)
        firsts = gather_columns(first)
        second = 0.0
        for j in (0, 1, 3, 2):
            second = second + dot(
                firsts[j], ordered[j * quarter_rows : (j + 1) * quarter_rows]
            )
        linear = 1.875 * current.astype(F32)
        if turn_index == 0:
            linear = linear * scale
        updated = linear - 1.25 * first.astype(F32) + 0.375 * second
        current = updated.astype(BF)

    final = (updated * math.sqrt(ROWS)).astype(BF)
    pixels = final.shape[1] // 2
    parts = final.reshape(half, 2, 16, pixels // 16).transpose(2, 3, 1, 0)
    parts = lax.all_to_all(parts, ("y", "xhi", "core"), split_axis=0, concat_axis=0, tiled=True)
    parts = parts.reshape(4, 2, 2, pixels // 16, 2, half).transpose(3, 0, 4, 2, 1, 5)
    return parts.reshape(pixels // 16, 16, 2 * half)


def solution(mesh):
    wide = Mesh(mesh.devices.reshape(2, 4, 4, 2, 2), AXES)
    return jax.shard_map(
        local,
        mesh=wide,
        in_specs=(P(("xlo", "z"), ("y", "xhi", "core")),),
        out_specs=P(("y", "xhi", "core"), None, ("xlo", "z")),
        check_vma=False,
    )
```
